32 devices in a mesh: mem: 8 (over z, core), reg: 4 (over y, x).
Axes of the slice: x: 2, y: 2, z: 4, core: 2. Of those that a mesh axis runs over, the one named last changes fastest.
Arguments:
- anomalies: bfloat16 [1024, 65536], P('mem', 'reg'), may hold values from -6 to 6
- obs_anomalies: bfloat16 [1024, 2048], P('mem', 'reg'), may hold values from -6 to 6
- innovations: bfloat16 [1024, 2048], P('mem', 'reg'), may hold values from -6 to 6
- obs_links: int32 [512, 12], P('reg'), may hold values from 0 to 19, as said below
- taper_choice: int32 [512, 12], P('reg'), may hold values from 0 to 7
- tapers: float32 [8, 128, 128], replicated, may hold values from 0.1 to 1
Outputs:
- increments: bfloat16 [1024, 65536], P('mem', 'reg')
The draws below stay inside these ranges and needn't reach their ends.
Inputs may be any that keep to these rules, and one draw needn't show every extreme that they name: `obs_links`: each row names 12 different positions of a window of 20 observation blocks: position w is block w mod 4 of region r + w // 4 - 2 (regions counted cyclically), r being the state block's region.
All inputs are finite; a program needn't handle non-finite values.
Results may differ from the reference program's by a relative error of at most 0.005.
Values may be sent and summed in bfloat16 or wider, within the bound.
A program may use at most 128 MiB of HBM per device.

```python
import jax
import jax.numpy as jnp
from jax import lax

MEMBERS = 1024
BLK = 128
LINKS = 12
NTAPER = 8
SBLK_REG = 128
OBLK_REG = 4
NSB = 512
NOB = 16
NSTATE = 65536
NOBS = 2048


def draw_obs_links(key, part):
    window_len = 5 * OBLK_REG
    row_keys = jax.random.split(key, NSB)
    scores = jax.vmap(lambda row_key: jax.random.permutation(row_key, window_len))(row_keys).astype(jnp.int32)
    scores = scores.at[0, 0].set(-2).at[0, window_len - 1].set(-1)
    ranking = jnp.argsort(scores, axis=1, stable=True)
    return ranking[:, :LINKS].astype(jnp.int32)


def plant(drawn, stream_key, least, high):
    dims = drawn.shape
    place = [jax.random.randint(jax.random.fold_in(stream_key, axis), (), 0, dims[axis]) for axis in range(len(dims))]
    drawn = drawn.at[tuple(place)].set(least)
    longest = dims.index(max(dims))
    place[longest] = (place[longest] + 1) % dims[longest]
    return drawn.at[tuple(place)].set(high)


def shard_levels(key, dims, pieces, low, largest):
    level, own = 1.0, jax.random.fold_in(key, 6)
    for dim, blocks in pieces:
        heights = jnp.exp(jax.random.uniform(jax.random.fold_in(own, dim), (blocks,), jnp.float32, low / len(pieces), largest / len(pieces)))
        level = level * jnp.repeat(heights, dims[dim] // blocks).reshape([-1 if axis == dim else 1 for axis in range(len(dims))])
    return level


def bell_draw(rng, extent, width, limit, pieces=(), held_as=jnp.bfloat16):
    entries = jax.random.normal(rng, extent, jnp.float32) * width
    if len(pieces) > 0:
        entries = shard_levels(rng, extent, pieces, -0.22, 0.18) * entries
    return jnp.clip(entries, min=-limit, max=limit).astype(held_as)


def setup_inputs(seed: int = 0) -> dict:
    arg_keys = jax.random.split(jax.random.key(seed), 7)
    return {
        "anomalies": bell_draw(arg_keys[0], (MEMBERS, NSTATE), 1.0, 6.0, ((0, 8), (1, 4))),
        "obs_anomalies": bell_draw(arg_keys[1], (MEMBERS, NOBS), 1.0, 6.0, ((0, 8), (1, 4))),
        "innovations": bell_draw(arg_keys[2], (MEMBERS, NOBS), 1.0, 6.0, ((0, 8), (1, 4))),
        "obs_links": draw_obs_links(jax.random.fold_in(arg_keys[6], 71), 0),
        "taper_choice": plant(jax.random.randint(arg_keys[4], (NSB, LINKS), 0, NTAPER), jax.random.fold_in(arg_keys[4], 1), 0, NTAPER - 1).astype(jnp.int32),
        "tapers": jnp.clip(jax.random.uniform(arg_keys[5], (NTAPER, BLK, BLK), jnp.float32, 0.1, 1.0), 0.1, 1.0),
    }


def reference(anomalies, obs_anomalies, innovations, obs_links, taper_choice, tapers):
    region = jnp.arange(NSB, dtype=jnp.int32) // SBLK_REG
    global_ids = ((region[:, None] * OBLK_REG - 2 * OBLK_REG + obs_links) % NOB).astype(jnp.int32)
    state_blocks = anomalies.reshape(MEMBERS, NSB, BLK)
    obs_blocks = obs_anomalies.reshape(MEMBERS, NOB, BLK)
    innov_blocks = innovations.reshape(MEMBERS, NOB, BLK)

    def single_block(block_index):
        state_block = lax.dynamic_index_in_dim(state_blocks, block_index, 1, keepdims=False).astype(jnp.float32)
        chosen_ids = global_ids[block_index]
        chosen_obs = jnp.take(obs_blocks, chosen_ids, axis=1).reshape(MEMBERS, LINKS * BLK).astype(jnp.float32)
        chosen_innov = jnp.take(innov_blocks, chosen_ids, axis=1).reshape(MEMBERS, LINKS * BLK).astype(jnp.float32)
        covariance = jnp.dot(state_block.T, chosen_obs, preferred_element_type=jnp.float32) / (MEMBERS - 1)
        taper_tiles = jnp.take(tapers, taper_choice[block_index], axis=0).transpose(1, 0, 2).reshape(BLK, LINKS * BLK)
        tapered = lax.optimization_barrier((covariance * taper_tiles).astype(jnp.bfloat16))
        return jnp.dot(chosen_innov, tapered.astype(jnp.float32).T, preferred_element_type=jnp.float32).astype(jnp.bfloat16)

    result = lax.map(single_block, jnp.arange(NSB, dtype=jnp.int32))
    return result.transpose(1, 0, 2).reshape(MEMBERS, NSB * BLK)
```

```python
import functools

import jax
import jax.numpy as jnp
from jax import lax
from jax.experimental import pallas as pl
from jax.experimental.pallas import tpu as pltpu
from jax.sharding import PartitionSpec as P

BLK = 128
REACH = 2
CORES = 2
MESH = pl.DeviceIdType.MESH


def wait_for(ref, sem):
    pltpu.make_async_copy(ref, ref, sem).wait()


def kernel(
    mem_count,
    reg_count,
    chunk,
    slots,
    steps,
    index_ref,
    taper_ref,
    anomalies,
    obs,
    innov,
    out,
    patches,
    window,
    turned,
    weighted,
    results,
    patch_send,
    patch_recv,
    out_send,
    out_recv,
    line_send,
    line_recv,
    pair_send,
    pair_recv,
    plane_send,
    plane_recv,
):
    mem = lax.axis_index("mem")
    reg = lax.axis_index("reg")
    chips = mem_count // CORES
    chip = mem // CORES
    core = lax.rem(mem, CORES)
    twin = chip * CORES + (1 - core)
    mem_dev = anomalies.shape[0]
    chunks = patches.shape[0]
    own_cols = chunks * chunk
    groups = window.shape[5] // BLK
    home = REACH % reg_count
    mem_order = sorted(range(1, mem_count), key=lambda by: abs(by - mem_count // 2))
    mine = pl.ds(pl.multiple_of(mem * mem_dev, mem_dev), mem_dev)

    def device(by):
        return lax.rem(mem + by, mem_count)

    def region(step):
        return lax.rem(reg + step + reg_count, reg_count)

    barrier = pltpu.get_barrier_semaphore()
    for by in range(1, mem_count):
        pl.semaphore_signal(barrier, inc=1, device_id=(device(by), reg), device_id_type=MESH)
    for step in steps:
        pl.semaphore_signal(barrier, inc=1, device_id=(mem, region(step)), device_id_type=MESH)
    pl.semaphore_wait(barrier, mem_count - 1 + len(steps))

    for kind, shard in ((0, obs), (1, innov)):
        there = window.at[home, kind, chip, core]
        for by in range(1, chips):
            peer = lax.rem(chip + by, chips) * CORES + core
            pltpu.make_async_remote_copy(
                shard, there, line_send, line_recv, device_id=(peer, reg), device_id_type=MESH
            ).start()
        pltpu.make_async_copy(shard, there, line_recv).start()

    def send_patches(c, carry):
        there = patches.at[c, mine]
        for by in mem_order:
            peer = device(by)
            first = pl.multiple_of(peer * own_cols + c * chunk, chunk)
            pltpu.make_async_remote_copy(
                anomalies.at[:, pl.ds(first, chunk)],
                there,
                patch_send,
                patch_recv.at[c],
                device_id=(peer, reg),
                device_id_type=MESH,
            ).start()
        first = pl.multiple_of(mem * own_cols + c * chunk, chunk)
        pltpu.make_async_copy(anomalies.at[:, pl.ds(first, chunk)], there, patch_recv.at[c]).start()
        return carry

    early = max(1, chunks // 8)
    middle = max(early, chunks * 5 // 8)
    lax.fori_loop(0, early, send_patches, 0)

    def share(slot):
        return window.at[slot, :, :, core]

    def other(slot):
        return window.at[slot, :, :, 1 - core]

    def to_twin(slot):
        pltpu.make_async_remote_copy(
            share(slot),
            share(slot),
            pair_send.at[slot],
            pair_recv.at[slot],
            device_id=(twin, reg),
            device_id_type=MESH,
        ).start()

    wait_for(share(home), line_recv)
    for step in steps:
        slot = (REACH - step) % reg_count
        pltpu.make_async_remote_copy(
            share(home),
            share(slot),
            plane_send.at[slot],
            plane_recv.at[slot],
            device_id=(mem, region(step)),
            device_id_type=MESH,
        ).start()
    to_twin(home)
    lax.fori_loop(early, middle, send_patches, 0)
    for step in steps:
        slot = (REACH - step) % reg_count
        wait_for(share(slot), plane_recv.at[slot])
        to_twin(slot)
    lax.fori_loop(middle, chunks, send_patches, 0)
    for slot in range(slots):
        wait_for(other(slot), pair_recv.at[slot])

    members = mem_count * mem_dev
    rows = min(256, members)
    positions = (2 * REACH + 1) * groups

    def analyse(c, carry):
        wait_for(patches.at[c], patch_recv.at[c])
        turned[...] = patches[c].T
        for slot in range(slots):
            cov = jnp.dot(
                turned[...],
                window[slot, 0].reshape(members, groups * BLK),
                preferred_element_type=jnp.float32,
            )
            for part in range(chunk // BLK):
                for group in range(groups):
                    tile = None
                    for w in range(slot * groups + group, positions, reg_count * groups):
                        one = taper_ref[index_ref[c * (chunk // BLK) + part, w]]
                        tile = one if tile is None else tile + one
                    piece = cov[part * BLK : (part + 1) * BLK, group * BLK : (group + 1) * BLK]
                    weighted[
                        slot, part * BLK : (part + 1) * BLK, group * BLK : (group + 1) * BLK
                    ] = (piece * tile).astype(jnp.bfloat16)
        flat = [window.at[slot, 1] for slot in range(slots)]
        per_chip = CORES * mem_dev
        for k in range(chips):
            total = None
            for slot in range(slots):
                term = lax.dot_general(
                    flat[slot][k].reshape(per_chip, groups * BLK),
                    weighted[slot],
                    (((1,), (1,)), ((), ())),
                    preferred_element_type=jnp.float32,
                )
                total = term if total is None else total + term
            results[c, k * per_chip : (k + 1) * per_chip, :] = total.astype(jnp.bfloat16)
        there = out.at[:, pl.ds(pl.multiple_of(mem * own_cols + c * chunk, chunk), chunk)]
        for by in mem_order:
            peer = device(by)
            pltpu.make_async_remote_copy(
                results.at[c, pl.ds(pl.multiple_of(peer * mem_dev, mem_dev), mem_dev)],
                there,
                out_send,
                out_recv,
                device_id=(peer, reg),
                device_id_type=MESH,
            ).start()
        pltpu.make_async_copy(results.at[c, mine], there, out_recv).start()
        return carry

    lax.fori_loop(0, chunks, analyse, 0)

    wait_for(out, out_recv)
    sent = pl.ds(0, (mem_count - 1) * own_cols)
    wait_for(anomalies.at[:, sent], patch_send)
    wait_for(out.at[:, sent], out_send)
    wait_for(window.at[home, :, 0 : chips - 1, 0], line_send)
    for slot in range(slots):
        wait_for(share(slot), pair_send.at[slot])
        if slot != home:
            wait_for(share(home), plane_send.at[slot])


def local(anomalies, obs_anomalies, innovations, obs_links, taper_choice, tapers):
    mem_dev, state_cols = anomalies.shape
    mem_count = lax.axis_size("mem")
    reg_count = lax.axis_size("reg")
    members = mem_dev * mem_count
    per_dev = state_cols // BLK // mem_count
    pair = 2 if per_dev % 2 == 0 else 1
    chunk = pair * BLK
    chunks = per_dev // pair
    obs_cols = obs_anomalies.shape[1]
    positions = (2 * REACH + 1) * obs_cols // BLK
    slots = min(2 * REACH + 1, reg_count)
    home = REACH % reg_count
    steps = [(REACH - slot) for slot in range(slots) if slot != home]
    first_block = lax.axis_index("mem") * per_dev
    my_links = lax.dynamic_slice_in_dim(obs_links, first_block, per_dev, 0)
    my_choice = lax.dynamic_slice_in_dim(taper_choice, first_block, per_dev, 0)
    position_ids = jnp.arange(positions, dtype=jnp.int32)
    linked = my_links[:, :, None] == position_ids[None, None, :]
    index = jnp.sum(jnp.where(linked, my_choice[:, :, None] + 1, 0), axis=1).astype(jnp.int32)
    tiles = jnp.concatenate([jnp.zeros((1, BLK, BLK), jnp.float32), tapers]) / (members - 1)
    DMA = pltpu.SemaphoreType.DMA
    chips = mem_count // CORES
    return pl.pallas_call(
        functools.partial(kernel, mem_count, reg_count, chunk, slots, steps),
        out_shape=jax.ShapeDtypeStruct((mem_dev, state_cols), jnp.bfloat16),
        in_specs=[
            pl.BlockSpec(memory_space=pltpu.SMEM),
            pl.BlockSpec(memory_space=pltpu.VMEM),
            pl.BlockSpec(memory_space=pl.ANY),
            pl.BlockSpec(memory_space=pl.ANY),
            pl.BlockSpec(memory_space=pl.ANY),
        ],
        out_specs=pl.BlockSpec(memory_space=pl.ANY),
        scratch_shapes=[
            pltpu.VMEM((chunks, members, chunk), jnp.bfloat16),
            pltpu.VMEM((slots, 2, chips, CORES, mem_dev, obs_cols), jnp.bfloat16),
            pltpu.VMEM((chunk, members), jnp.bfloat16),
            pltpu.VMEM((slots, chunk, obs_cols), jnp.bfloat16),
            pltpu.VMEM((chunks, members, chunk), jnp.bfloat16),
            DMA,
            DMA((chunks,)),
            DMA,
            DMA,
            DMA,
            DMA,
            DMA((slots,)),
            DMA((slots,)),
            DMA((slots,)),
            DMA((slots,)),
        ],
        compiler_params=pltpu.CompilerParams(
            collective_id=0, has_side_effects=True, vmem_limit_bytes=48 * 1024 * 1024
        ),
        cost_estimate=pl.CostEstimate(
            flops=4 * members * per_dev * BLK * slots * obs_cols,
            bytes_accessed=4 * mem_dev * state_cols * 2,
            transcendentals=0,
        ),
    )(index, tiles, anomalies, obs_anomalies, innovations)


def solution(mesh):
    return jax.shard_map(
        local,
        mesh=mesh,
        in_specs=(
            P("mem", "reg"),
            P("mem", "reg"),
            P("mem", "reg"),
            P("reg", None),
            P("reg", None),
            P(),
        ),
        out_specs=P("mem", "reg"),
        check_vma=False,
    )
```

```python
import functools

import jax
import jax.numpy as jnp
from jax import lax
from jax.experimental import pallas as pl
from jax.experimental.pallas import tpu as pltpu
from jax.sharding import PartitionSpec as P

BLK = 128
REACH = 2
CORES = 2
MESH = pl.DeviceIdType.MESH


def wait_for(ref, sem):
    pltpu.make_async_copy(ref, ref, sem).wait()


def kernel(
    mem_count,
    reg_count,
    chunk,
    slots,
    steps,
    index_ref,
    tapers,
    anomalies,
    obs,
    innov,
    out,
    patches,
    window,
    tiles,
    turned,
    weighted,
    results,
    patch_send,
    patch_recv,
    out_send,
    out_recv,
    line_send,
    line_recv,
    pair_send,
    pair_recv,
    plane_send,
    plane_recv,
    tile_sem,
):
    mem = lax.axis_index("mem")
    reg = lax.axis_index("reg")
    chips = mem_count // CORES
    chip = mem // CORES
    core = lax.rem(mem, CORES)
    twin = chip * CORES + (1 - core)
    mem_dev = anomalies.shape[0]
    chunks = patches.shape[0]
    own_cols = chunks * chunk
    groups = window.shape[5] // BLK
    home = REACH % reg_count
    mem_order = sorted(range(1, mem_count), key=lambda by: abs(by - mem_count // 2))
    mine = pl.ds(pl.multiple_of(mem * mem_dev, mem_dev), mem_dev)

    def device(by):
        return lax.rem(mem + by, mem_count)

    def region(step):
        return lax.rem(reg + step + reg_count, reg_count)

    load = pltpu.make_async_copy(tapers, tiles.at[pl.ds(1, tapers.shape[0])], tile_sem)
    load.start()
    barrier = pltpu.get_barrier_semaphore()
    for by in range(1, mem_count):
        pl.semaphore_signal(barrier, inc=1, device_id=(device(by), reg), device_id_type=MESH)
    for step in steps:
        pl.semaphore_signal(barrier, inc=1, device_id=(mem, region(step)), device_id_type=MESH)
    pl.semaphore_wait(barrier, mem_count - 1 + len(steps))

    def send_patches(c, carry):
        there = patches.at[c, mine]
        for by in mem_order:
            peer = device(by)
            first = pl.multiple_of(peer * own_cols + c * chunk, chunk)
            pltpu.make_async_remote_copy(
                anomalies.at[:, pl.ds(first, chunk)],
                there,
                patch_send,
                patch_recv.at[c],
                device_id=(peer, reg),
                device_id_type=MESH,
            ).start()
        first = pl.multiple_of(mem * own_cols + c * chunk, chunk)
        pltpu.make_async_copy(anomalies.at[:, pl.ds(first, chunk)], there, patch_recv.at[c]).start()
        return carry

    def flipped(mask):
        at = chip
        bit = 1
        while bit < chips:
            if mask & bit:
                at = at + bit * (1 - 2 * lax.rem(at // bit, 2))
            bit *= 2
        return at

    issued = 0
    held = [0]
    for kind, shard in ((0, obs), (1, innov)):
        pltpu.make_async_copy(shard, window.at[home, kind, chip, core], line_recv.at[0]).start()
    bit = chips // 2
    while bit >= 1:
        peer = flipped(bit) * CORES + core
        for mask in held:
            for kind, shard in ((0, obs), (1, innov)):
                there = window.at[home, kind, flipped(mask), core]
                pltpu.make_async_remote_copy(
                    there if mask else shard,
                    there,
                    line_send,
                    line_recv.at[mask + bit],
                    device_id=(peer, reg),
                    device_id_type=MESH,
                ).start()
        if issued < chunks:
            send_patches(issued, 0)
            issued += 1
        if bit == chips // 2:
            load.wait()
            tiles[0] = jnp.zeros_like(tiles[0])
            for t in range(tapers.shape[0]):
                tiles[t + 1] = tiles[t + 1] / (mem_count * mem_dev - 1)
        came = [mask + bit for mask in held]
        for mask in came:
            wait_for(window.at[home, :, flipped(mask), core], line_recv.at[mask])
        held = held + came
        bit //= 2
    wait_for(window.at[home, :, chip, core], line_recv.at[0])
    middle = max(issued, chunks * 5 // 8)

    def share(slot):
        return window.at[slot, :, :, core]

    def other(slot):
        return window.at[slot, :, :, 1 - core]

    def to_twin(slot):
        pltpu.make_async_remote_copy(
            share(slot),
            share(slot),
            pair_send.at[slot],
            pair_recv.at[slot],
            device_id=(twin, reg),
            device_id_type=MESH,
        ).start()

    for step in steps:
        slot = (REACH - step) % reg_count
        pltpu.make_async_remote_copy(
            share(home),
            share(slot),
            plane_send.at[slot],
            plane_recv.at[slot],
            device_id=(mem, region(step)),
            device_id_type=MESH,
        ).start()
    to_twin(home)
    lax.fori_loop(issued, middle, send_patches, 0)
    for step in steps:
        slot = (REACH - step) % reg_count
        wait_for(share(slot), plane_recv.at[slot])
        to_twin(slot)
    lax.fori_loop(middle, chunks, send_patches, 0)
    for slot in range(slots):
        wait_for(other(slot), pair_recv.at[slot])

    members = mem_count * mem_dev
    rows = min(256, members)
    positions = (2 * REACH + 1) * groups

    def analyse(c, carry):
        wait_for(patches.at[c], patch_recv.at[c])
        turned[...] = patches[c].T
        for slot in range(slots):
            cov = jnp.dot(
                turned[...],
                window[slot, 0].reshape(members, groups * BLK),
                preferred_element_type=jnp.float32,
            )
            for part in range(chunk // BLK):
                for group in range(groups):
                    tile = None
                    for w in range(slot * groups + group, positions, reg_count * groups):
                        one = tiles[index_ref[c * (chunk // BLK) + part, w]]
                        tile = one if tile is None else tile + one
                    piece = cov[part * BLK : (part + 1) * BLK, group * BLK : (group + 1) * BLK]
                    weighted[
                        slot, part * BLK : (part + 1) * BLK, group * BLK : (group + 1) * BLK
                    ] = (piece * tile).astype(jnp.bfloat16)
        flat = [window.at[slot, 1] for slot in range(slots)]
        per_chip = CORES * mem_dev
        for k in range(chips):
            total = None
            for slot in range(slots):
                term = lax.dot_general(
                    flat[slot][k].reshape(per_chip, groups * BLK),
                    weighted[slot],
                    (((1,), (1,)), ((), ())),
                    preferred_element_type=jnp.float32,
                )
                total = term if total is None else total + term
            results[c, k * per_chip : (k + 1) * per_chip, :] = total.astype(jnp.bfloat16)
        there = out.at[:, pl.ds(pl.multiple_of(mem * own_cols + c * chunk, chunk), chunk)]
        for by in mem_order:
            peer = device(by)
            pltpu.make_async_remote_copy(
                results.at[c, pl.ds(pl.multiple_of(peer * mem_dev, mem_dev), mem_dev)],
                there,
                out_send,
                out_recv,
                device_id=(peer, reg),
                device_id_type=MESH,
            ).start()
        pltpu.make_async_copy(results.at[c, mine], there, out_recv).start()
        return carry

    lax.fori_loop(0, chunks, analyse, 0)

    wait_for(out, out_recv)
    sent = pl.ds(0, (mem_count - 1) * own_cols)
    wait_for(anomalies.at[:, sent], patch_send)
    wait_for(out.at[:, sent], out_send)
    wait_for(window.at[home, :, 0 : chips - 1, 0], line_send)
    for slot in range(slots):
        wait_for(share(slot), pair_send.at[slot])
        if slot != home:
            wait_for(share(home), plane_send.at[slot])


def local(anomalies, obs_anomalies, innovations, obs_links, taper_choice, tapers):
    mem_dev, state_cols = anomalies.shape
    mem_count = lax.axis_size("mem")
    reg_count = lax.axis_size("reg")
    members = mem_dev * mem_count
    per_dev = state_cols // BLK // mem_count
    pair = 2 if per_dev % 2 == 0 else 1
    chunk = pair * BLK
    chunks = per_dev // pair
    obs_cols = obs_anomalies.shape[1]
    positions = (2 * REACH + 1) * obs_cols // BLK
    slots = min(2 * REACH + 1, reg_count)
    home = REACH % reg_count
    steps = [(REACH - slot) for slot in range(slots) if slot != home]
    first_block = lax.axis_index("mem") * per_dev
    my_links = lax.dynamic_slice_in_dim(obs_links, first_block, per_dev, 0)
    my_choice = lax.dynamic_slice_in_dim(taper_choice, first_block, per_dev, 0)
    position_ids = jnp.arange(positions, dtype=jnp.int32)
    linked = my_links[:, :, None] == position_ids[None, None, :]
    index = jnp.sum(jnp.where(linked, my_choice[:, :, None] + 1, 0), axis=1).astype(jnp.int32)
    DMA = pltpu.SemaphoreType.DMA
    chips = mem_count // CORES
    return pl.pallas_call(
        functools.partial(kernel, mem_count, reg_count, chunk, slots, steps),
        out_shape=jax.ShapeDtypeStruct((mem_dev, state_cols), jnp.bfloat16),
        in_specs=[
            pl.BlockSpec(memory_space=pltpu.SMEM),
            pl.BlockSpec(memory_space=pltpu.HBM),
            pl.BlockSpec(memory_space=pltpu.HBM),
            pl.BlockSpec(memory_space=pltpu.HBM),
            pl.BlockSpec(memory_space=pltpu.HBM),
        ],
        out_specs=pl.BlockSpec(memory_space=pl.ANY),
        scratch_shapes=[
            pltpu.VMEM((chunks, members, chunk), jnp.bfloat16),
            pltpu.VMEM((slots, 2, chips, CORES, mem_dev, obs_cols), jnp.bfloat16),
            pltpu.VMEM((tapers.shape[0] + 1, BLK, BLK), jnp.float32),
            pltpu.VMEM((chunk, members), jnp.bfloat16),
            pltpu.VMEM((slots, chunk, obs_cols), jnp.bfloat16),
            pltpu.VMEM((chunks, members, chunk), jnp.bfloat16),
            DMA,
            DMA((chunks,)),
            DMA,
            DMA,
            DMA,
            DMA((chips,)),
            DMA((slots,)),
            DMA((slots,)),
            DMA((slots,)),
            DMA((slots,)),
            DMA,
        ],
        compiler_params=pltpu.CompilerParams(
            collective_id=0, has_side_effects=True, vmem_limit_bytes=56 * 1024 * 1024
        ),
        cost_estimate=pl.CostEstimate(
            flops=4 * members * per_dev * BLK * slots * obs_cols,
            bytes_accessed=4 * mem_dev * state_cols * 2,
            transcendentals=0,
        ),
    )(index, tapers, anomalies, obs_anomalies, innovations)


def solution(mesh):
    return jax.shard_map(
        local,
        mesh=mesh,
        in_specs=(
            P("mem", "reg"),
            P("mem", "reg"),
            P("mem", "reg"),
            P("reg", None),
            P("reg", None),
            P(),
        ),
        out_specs=P("mem", "reg"),
        check_vma=False,
    )
```

```python
import functools

import jax
import jax.numpy as jnp
from jax import lax
from jax.experimental import pallas as pl
from jax.experimental.pallas import tpu as pltpu
from jax.sharding import PartitionSpec as P

BLK = 128
REACH = 2
CORES = 2
MESH = pl.DeviceIdType.MESH


def wait_for(ref, sem):
    pltpu.make_async_copy(ref, ref, sem).wait()


def kernel(
    mem_count,
    reg_count,
    chunk,
    slots,
    steps,
    index_ref,
    tapers,
    anomalies,
    obs,
    innov,
    out,
    patches,
    window,
    tiles,
    turned,
    weighted,
    results,
    patch_send,
    patch_recv,
    out_send,
    out_recv,
    line_send,
    line_recv,
    pair_send,
    pair_recv,
    plane_send,
    plane_recv,
    tile_sem,
):
    mem = lax.axis_index("mem")
    reg = lax.axis_index("reg")
    chips = mem_count // CORES
    chip = mem // CORES
    core = lax.rem(mem, CORES)
    twin = chip * CORES + (1 - core)
    mem_dev = anomalies.shape[0]
    chunks = patches.shape[0]
    own_cols = chunks * chunk
    groups = window.shape[5] // BLK
    home = REACH % reg_count
    mem_order = sorted(range(1, mem_count), key=lambda by: abs(by - mem_count // 2))
    mine = pl.ds(pl.multiple_of(mem * mem_dev, mem_dev), mem_dev)

    def device(by):
        return lax.rem(mem + by, mem_count)

    def region(step):
        return lax.rem(reg + step + reg_count, reg_count)

    load = pltpu.make_async_copy(tapers, tiles.at[pl.ds(1, tapers.shape[0])], tile_sem)
    load.start()
    barrier = pltpu.get_barrier_semaphore()
    for by in range(1, mem_count):
        pl.semaphore_signal(barrier, inc=1, device_id=(device(by), reg), device_id_type=MESH)
    for step in steps:
        pl.semaphore_signal(barrier, inc=1, device_id=(mem, region(step)), device_id_type=MESH)
    pl.semaphore_wait(barrier, mem_count - 1 + len(steps))

    def send_patches(c, carry):
        there = patches.at[c, mine]
        for by in mem_order:
            peer = device(by)
            first = pl.multiple_of(peer * own_cols + c * chunk, chunk)
            pltpu.make_async_remote_copy(
                anomalies.at[:, pl.ds(first, chunk)],
                there,
                patch_send,
                patch_recv.at[c],
                device_id=(peer, reg),
                device_id_type=MESH,
            ).start()
        first = pl.multiple_of(mem * own_cols + c * chunk, chunk)
        pltpu.make_async_copy(anomalies.at[:, pl.ds(first, chunk)], there, patch_recv.at[c]).start()
        return carry

    def flipped(mask):
        at = chip
        bit = 1
        while bit < chips:
            if mask & bit:
                at = at + bit * (1 - 2 * lax.rem(at // bit, 2))
            bit *= 2
        return at

    def to_plane(mask):
        for step in steps:
            slot = (REACH - step) % reg_count
            if mask:
                pieces = [window.at[home, :, flipped(mask), core]]
                places = [window.at[slot, :, flipped(mask), core]]
            else:
                pieces = [obs, innov]
                places = [window.at[slot, kind, chip, core] for kind in (0, 1)]
            for piece, place in zip(pieces, places):
                pltpu.make_async_remote_copy(
                    piece,
                    place,
                    plane_send.at[slot],
                    plane_recv.at[slot],
                    device_id=(mem, region(step)),
                    device_id_type=MESH,
                ).start()

    issued = 0
    held = [0]
    fresh = [0]
    for kind, shard in ((0, obs), (1, innov)):
        pltpu.make_async_copy(shard, window.at[home, kind, chip, core], line_recv.at[0]).start()
    bit = chips // 2
    while bit >= 1:
        peer = flipped(bit) * CORES + core
        for mask in held:
            for kind, shard in ((0, obs), (1, innov)):
                there = window.at[home, kind, flipped(mask), core]
                pltpu.make_async_remote_copy(
                    there if mask else shard,
                    there,
                    line_send,
                    line_recv.at[mask + bit],
                    device_id=(peer, reg),
                    device_id_type=MESH,
                ).start()
        for mask in fresh:
            to_plane(mask)
        if issued < chunks:
            send_patches(issued, 0)
            issued += 1
        if bit == chips // 2:
            load.wait()
            tiles[0] = jnp.zeros_like(tiles[0])
            for t in range(tapers.shape[0]):
                tiles[t + 1] = tiles[t + 1] / (mem_count * mem_dev - 1)
        came = [mask + bit for mask in held]
        for mask in came:
            wait_for(window.at[home, :, flipped(mask), core], line_recv.at[mask])
        held = held + came
        fresh = came
        bit //= 2
    wait_for(window.at[home, :, chip, core], line_recv.at[0])
    for mask in fresh:
        to_plane(mask)
    middle = max(issued, chunks * 6 // 8)

    def share(slot):
        return window.at[slot, :, :, core]

    def other(slot):
        return window.at[slot, :, :, 1 - core]

    def to_twin(slot):
        pltpu.make_async_remote_copy(
            share(slot),
            share(slot),
            pair_send.at[slot],
            pair_recv.at[slot],
            device_id=(twin, reg),
            device_id_type=MESH,
        ).start()

    to_twin(home)
    lax.fori_loop(issued, middle, send_patches, 0)
    for step in steps:
        slot = (REACH - step) % reg_count
        wait_for(share(slot), plane_recv.at[slot])
        to_twin(slot)
    lax.fori_loop(middle, chunks, send_patches, 0)
    for slot in range(slots):
        wait_for(other(slot), pair_recv.at[slot])

    members = mem_count * mem_dev
    rows = min(256, members)
    positions = (2 * REACH + 1) * groups

    def analyse(c, carry):
        wait_for(patches.at[c], patch_recv.at[c])
        turned[...] = patches[c].T
        for slot in range(slots):
            cov = jnp.dot(
                turned[...],
                window[slot, 0].reshape(members, groups * BLK),
                preferred_element_type=jnp.float32,
            )
            for part in range(chunk // BLK):
                for group in range(groups):
                    tile = None
                    for w in range(slot * groups + group, positions, reg_count * groups):
                        one = tiles[index_ref[c * (chunk // BLK) + part, w]]
                        tile = one if tile is None else tile + one
                    piece = cov[part * BLK : (part + 1) * BLK, group * BLK : (group + 1) * BLK]
                    weighted[
                        slot, part * BLK : (part + 1) * BLK, group * BLK : (group + 1) * BLK
                    ] = (piece * tile).astype(jnp.bfloat16)
        flat = [window.at[slot, 1] for slot in range(slots)]
        per_chip = CORES * mem_dev
        for k in range(chips):
            total = None
            for slot in range(slots):
                term = lax.dot_general(
                    flat[slot][k].reshape(per_chip, groups * BLK),
                    weighted[slot],
                    (((1,), (1,)), ((), ())),
                    preferred_element_type=jnp.float32,
                )
                total = term if total is None else total + term
            results[c, k * per_chip : (k + 1) * per_chip, :] = total.astype(jnp.bfloat16)
        there = out.at[:, pl.ds(pl.multiple_of(mem * own_cols + c * chunk, chunk), chunk)]
        for by in mem_order:
            peer = device(by)
            pltpu.make_async_remote_copy(
                results.at[c, pl.ds(pl.multiple_of(peer * mem_dev, mem_dev), mem_dev)],
                there,
                out_send,
                out_recv,
                device_id=(peer, reg),
                device_id_type=MESH,
            ).start()
        pltpu.make_async_copy(results.at[c, mine], there, out_recv).start()
        return carry

    lax.fori_loop(0, chunks, analyse, 0)

    wait_for(out, out_recv)
    sent = pl.ds(0, (mem_count - 1) * own_cols)
    wait_for(anomalies.at[:, sent], patch_send)
    wait_for(out.at[:, sent], out_send)
    wait_for(window.at[home, :, 0 : chips - 1, 0], line_send)
    for slot in range(slots):
        wait_for(share(slot), pair_send.at[slot])
        if slot != home:
            wait_for(share(home), plane_send.at[slot])


def local(anomalies, obs_anomalies, innovations, obs_links, taper_choice, tapers):
    mem_dev, state_cols = anomalies.shape
    mem_count = lax.axis_size("mem")
    reg_count = lax.axis_size("reg")
    members = mem_dev * mem_count
    per_dev = state_cols // BLK // mem_count
    pair = 2 if per_dev % 2 == 0 else 1
    chunk = pair * BLK
    chunks = per_dev // pair
    obs_cols = obs_anomalies.shape[1]
    positions = (2 * REACH + 1) * obs_cols // BLK
    slots = min(2 * REACH + 1, reg_count)
    home = REACH % reg_count
    steps = [(REACH - slot) for slot in range(slots) if slot != home]
    first_block = lax.axis_index("mem") * per_dev
    my_links = lax.dynamic_slice_in_dim(obs_links, first_block, per_dev, 0)
    my_choice = lax.dynamic_slice_in_dim(taper_choice, first_block, per_dev, 0)
    position_ids = jnp.arange(positions, dtype=jnp.int32)
    linked = my_links[:, :, None] == position_ids[None, None, :]
    index = jnp.sum(jnp.where(linked, my_choice[:, :, None] + 1, 0), axis=1).astype(jnp.int32)
    DMA = pltpu.SemaphoreType.DMA
    chips = mem_count // CORES
    return pl.pallas_call(
        functools.partial(kernel, mem_count, reg_count, chunk, slots, steps),
        out_shape=jax.ShapeDtypeStruct((mem_dev, state_cols), jnp.bfloat16),
        in_specs=[
            pl.BlockSpec(memory_space=pltpu.SMEM),
            pl.BlockSpec(memory_space=pltpu.HBM),
            pl.BlockSpec(memory_space=pltpu.HBM),
            pl.BlockSpec(memory_space=pltpu.HBM),
            pl.BlockSpec(memory_space=pltpu.HBM),
        ],
        out_specs=pl.BlockSpec(memory_space=pl.ANY),
        scratch_shapes=[
            pltpu.VMEM((chunks, members, chunk), jnp.bfloat16),
            pltpu.VMEM((slots, 2, chips, CORES, mem_dev, obs_cols), jnp.bfloat16),
            pltpu.VMEM((tapers.shape[0] + 1, BLK, BLK), jnp.float32),
            pltpu.VMEM((chunk, members), jnp.bfloat16),
            pltpu.VMEM((slots, chunk, obs_cols), jnp.bfloat16),
            pltpu.VMEM((chunks, members, chunk), jnp.bfloat16),
            DMA,
            DMA((chunks,)),
            DMA,
            DMA,
            DMA,
            DMA((chips,)),
            DMA((slots,)),
            DMA((slots,)),
            DMA((slots,)),
            DMA((slots,)),
            DMA,
        ],
        compiler_params=pltpu.CompilerParams(
            collective_id=0, has_side_effects=True, vmem_limit_bytes=56 * 1024 * 1024
        ),
        cost_estimate=pl.CostEstimate(
            flops=4 * members * per_dev * BLK * slots * obs_cols,
            bytes_accessed=4 * mem_dev * state_cols * 2,
            transcendentals=0,
        ),
    )(index, tapers, anomalies, obs_anomalies, innovations)


def solution(mesh):
    return jax.shard_map(
        local,
        mesh=mesh,
        in_specs=(
            P("mem", "reg"),
            P("mem", "reg"),
            P("mem", "reg"),
            P("reg", None),
            P("reg", None),
            P(),
        ),
        out_specs=P("mem", "reg"),
        check_vma=False,
    )
```

```python
import functools

import jax
import jax.numpy as jnp
from jax import lax
from jax.experimental import pallas as pl
from jax.experimental.pallas import tpu as pltpu
from jax.sharding import PartitionSpec as P

BLK = 128
REACH = 2
CORES = 2
MESH = pl.DeviceIdType.MESH


def wait_for(ref, sem):
    pltpu.make_async_copy(ref, ref, sem).wait()


def kernel(
    mem_count,
    reg_count,
    chunk,
    slots,
    steps,
    index_ref,
    tapers,
    anomalies,
    obs,
    innov,
    out,
    patches,
    window,
    tiles,
    turned,
    weighted,
    results,
    patch_send,
    patch_recv,
    out_send,
    out_recv,
    line_send,
    line_recv,
    pair_send,
    pair_recv,
    plane_send,
    plane_recv,
    tile_sem,
):
    mem = lax.axis_index("mem")
    reg = lax.axis_index("reg")
    chips = mem_count // CORES
    chip = mem // CORES
    core = lax.rem(mem, CORES)
    twin = chip * CORES + (1 - core)
    mem_dev = anomalies.shape[0]
    chunks = patches.shape[0]
    own_cols = chunks * chunk
    groups = window.shape[5] // BLK
    home = REACH % reg_count
    mem_order = sorted(range(1, mem_count), key=lambda by: abs(by - mem_count // 2))
    mine = pl.ds(pl.multiple_of(mem * mem_dev, mem_dev), mem_dev)

    def device(by):
        return lax.rem(mem + by, mem_count)

    def region(step):
        return lax.rem(reg + step + reg_count, reg_count)

    load = pltpu.make_async_copy(tapers, tiles.at[pl.ds(1, tapers.shape[0])], tile_sem)
    load.start()
    barrier = pltpu.get_barrier_semaphore()
    for by in range(1, mem_count):
        pl.semaphore_signal(barrier, inc=1, device_id=(device(by), reg), device_id_type=MESH)
    for step in steps:
        pl.semaphore_signal(barrier, inc=1, device_id=(mem, region(step)), device_id_type=MESH)
    pl.semaphore_wait(barrier, mem_count - 1 + len(steps))

    def send_patches(c, carry):
        there = patches.at[c, mine]
        for by in mem_order:
            peer = device(by)
            first = pl.multiple_of(peer * own_cols + c * chunk, chunk)
            pltpu.make_async_remote_copy(
                anomalies.at[:, pl.ds(first, chunk)],
                there,
                patch_send,
                patch_recv.at[c],
                device_id=(peer, reg),
                device_id_type=MESH,
            ).start()
        first = pl.multiple_of(mem * own_cols + c * chunk, chunk)
        pltpu.make_async_copy(anomalies.at[:, pl.ds(first, chunk)], there, patch_recv.at[c]).start()
        return carry

    def flipped(mask):
        at = chip
        bit = 1
        while bit < chips:
            if mask & bit:
                at = at + bit * (1 - 2 * lax.rem(at // bit, 2))
            bit *= 2
        return at

    relay = reg_count == 4
    if relay:
        across = {1: reg + 1 - 2 * lax.rem(reg, 2), 2: lax.rem(reg + 2, 4), 3: 3 - reg}

        def slot_at(receiver, source):
            return lax.rem(source - receiver + REACH + 4, 4)

        lanes = [
            (key, across[key], slot_at(across[key], reg), slot_at(reg, across[key]))
            for key in (1, 2)
        ]
        home_key = 0
    else:
        lanes = [
            ((REACH - step) % reg_count, region(step), (REACH - step) % reg_count, (REACH - step) % reg_count)
            for step in steps
        ]
        home_key = home

    def to_plane(mask):
        for key, there, slot, _ in lanes:
            if mask:
                pieces = [window.at[home, :, flipped(mask), core]]
                places = [window.at[slot, :, flipped(mask), core]]
            else:
                pieces = [obs, innov]
                places = [window.at[slot, kind, chip, core] for kind in (0, 1)]
            for piece, place in zip(pieces, places):
                pltpu.make_async_remote_copy(
                    piece,
                    place,
                    plane_send.at[key],
                    plane_recv.at[key],
                    device_id=(mem, there),
                    device_id_type=MESH,
                ).start()

    issued = 0
    held = [0]
    fresh = [0]
    for kind, shard in ((0, obs), (1, innov)):
        pltpu.make_async_copy(shard, window.at[home, kind, chip, core], line_recv.at[0]).start()
    bit = chips // 2
    while bit >= 1:
        peer = flipped(bit) * CORES + core
        for mask in held:
            for kind, shard in ((0, obs), (1, innov)):
                there = window.at[home, kind, flipped(mask), core]
                pltpu.make_async_remote_copy(
                    there if mask else shard,
                    there,
                    line_send,
                    line_recv.at[mask + bit],
                    device_id=(peer, reg),
                    device_id_type=MESH,
                ).start()
        for mask in fresh:
            to_plane(mask)
        if issued < chunks:
            send_patches(issued, 0)
            issued += 1
        if bit == chips // 2:
            load.wait()
            tiles[0] = jnp.zeros_like(tiles[0])
            for t in range(tapers.shape[0]):
                tiles[t + 1] = tiles[t + 1] / (mem_count * mem_dev - 1)
        came = [mask + bit for mask in held]
        for mask in came:
            wait_for(window.at[home, :, flipped(mask), core], line_recv.at[mask])
        held = held + came
        fresh = came
        bit //= 2
    wait_for(window.at[home, :, chip, core], line_recv.at[0])
    for mask in fresh:
        to_plane(mask)
    middle = max(issued, chunks * 6 // 8)

    def share(slot):
        return window.at[slot, :, :, core]

    def other(slot):
        return window.at[slot, :, :, 1 - core]

    def to_twin(slot, key):
        pltpu.make_async_remote_copy(
            share(slot),
            share(slot),
            pair_send.at[key],
            pair_recv.at[key],
            device_id=(twin, reg),
            device_id_type=MESH,
        ).start()

    to_twin(home, home_key)
    lax.fori_loop(issued, middle, send_patches, 0)
    for key, _, _, slot in lanes:
        wait_for(share(slot), plane_recv.at[key])
        if relay:
            onward, kind = 3 - key, 2 - key
            pltpu.make_async_remote_copy(
                window.at[slot, kind, :, core],
                window.at[slot_at(across[onward], across[key]), kind, :, core],
                plane_send.at[3],
                plane_recv.at[3],
                device_id=(mem, across[onward]),
                device_id_type=MESH,
            ).start()
        to_twin(slot, key)
    lax.fori_loop(middle, chunks, send_patches, 0)
    arrivals = [(home_key, home)] + [(key, slot) for key, _, _, slot in lanes]
    if relay:
        opposite = slot_at(reg, across[3])
        wait_for(share(opposite), plane_recv.at[3])
        to_twin(opposite, 3)
        arrivals.append((3, opposite))
    for key, slot in arrivals:
        wait_for(other(slot), pair_recv.at[key])

    members = mem_count * mem_dev
    positions = (2 * REACH + 1) * groups

    def analyse(c, carry):
        wait_for(patches.at[c], patch_recv.at[c])
        turned[...] = patches[c].T
        for slot in range(slots):
            cov = jnp.dot(
                turned[...],
                window[slot, 0].reshape(members, groups * BLK),
                preferred_element_type=jnp.float32,
            )
            for part in range(chunk // BLK):
                for group in range(groups):
                    tile = None
                    for w in range(slot * groups + group, positions, reg_count * groups):
                        one = tiles[index_ref[c * (chunk // BLK) + part, w]]
                        tile = one if tile is None else tile + one
                    piece = cov[part * BLK : (part + 1) * BLK, group * BLK : (group + 1) * BLK]
                    weighted[
                        slot, part * BLK : (part + 1) * BLK, group * BLK : (group + 1) * BLK
                    ] = (piece * tile).astype(jnp.bfloat16)
        flat = [window.at[slot, 1] for slot in range(slots)]
        per_chip = CORES * mem_dev
        for k in range(chips):
            total = None
            for slot in range(slots):
                term = lax.dot_general(
                    flat[slot][k].reshape(per_chip, groups * BLK),
                    weighted[slot],
                    (((1,), (1,)), ((), ())),
                    preferred_element_type=jnp.float32,
                )
                total = term if total is None else total + term
            results[c, k * per_chip : (k + 1) * per_chip, :] = total.astype(jnp.bfloat16)
        there = out.at[:, pl.ds(pl.multiple_of(mem * own_cols + c * chunk, chunk), chunk)]
        for by in mem_order:
            peer = device(by)
            pltpu.make_async_remote_copy(
                results.at[c, pl.ds(pl.multiple_of(peer * mem_dev, mem_dev), mem_dev)],
                there,
                out_send,
                out_recv,
                device_id=(peer, reg),
                device_id_type=MESH,
            ).start()
        pltpu.make_async_copy(results.at[c, mine], there, out_recv).start()
        return carry

    lax.fori_loop(0, chunks, analyse, 0)

    wait_for(out, out_recv)
    sent = pl.ds(0, (mem_count - 1) * own_cols)
    wait_for(anomalies.at[:, sent], patch_send)
    wait_for(out.at[:, sent], out_send)
    wait_for(window.at[home, :, 0 : chips - 1, 0], line_send)
    for key, _ in arrivals:
        wait_for(share(home), pair_send.at[key])
        if key != home_key:
            wait_for(share(home), plane_send.at[key])


def local(anomalies, obs_anomalies, innovations, obs_links, taper_choice, tapers):
    mem_dev, state_cols = anomalies.shape
    mem_count = lax.axis_size("mem")
    reg_count = lax.axis_size("reg")
    members = mem_dev * mem_count
    per_dev = state_cols // BLK // mem_count
    pair = 2 if per_dev % 2 == 0 else 1
    chunk = pair * BLK
    chunks = per_dev // pair
    obs_cols = obs_anomalies.shape[1]
    positions = (2 * REACH + 1) * obs_cols // BLK
    slots = min(2 * REACH + 1, reg_count)
    home = REACH % reg_count
    steps = [(REACH - slot) for slot in range(slots) if slot != home]
    first_block = lax.axis_index("mem") * per_dev
    my_links = lax.dynamic_slice_in_dim(obs_links, first_block, per_dev, 0)
    my_choice = lax.dynamic_slice_in_dim(taper_choice, first_block, per_dev, 0)
    position_ids = jnp.arange(positions, dtype=jnp.int32)
    linked = my_links[:, :, None] == position_ids[None, None, :]
    index = jnp.sum(jnp.where(linked, my_choice[:, :, None] + 1, 0), axis=1).astype(jnp.int32)
    DMA = pltpu.SemaphoreType.DMA
    chips = mem_count // CORES
    return pl.pallas_call(
        functools.partial(kernel, mem_count, reg_count, chunk, slots, steps),
        out_shape=jax.ShapeDtypeStruct((mem_dev, state_cols), jnp.bfloat16),
        in_specs=[
            pl.BlockSpec(memory_space=pltpu.SMEM),
            pl.BlockSpec(memory_space=pltpu.HBM),
            pl.BlockSpec(memory_space=pltpu.HBM),
            pl.BlockSpec(memory_space=pltpu.HBM),
            pl.BlockSpec(memory_space=pltpu.HBM),
        ],
        out_specs=pl.BlockSpec(memory_space=pl.ANY),
        scratch_shapes=[
            pltpu.VMEM((chunks, members, chunk), jnp.bfloat16),
            pltpu.VMEM((slots, 2, chips, CORES, mem_dev, obs_cols), jnp.bfloat16),
            pltpu.VMEM((tapers.shape[0] + 1, BLK, BLK), jnp.float32),
            pltpu.VMEM((chunk, members), jnp.bfloat16),
            pltpu.VMEM((slots, chunk, obs_cols), jnp.bfloat16),
            pltpu.VMEM((chunks, members, chunk), jnp.bfloat16),
            DMA,
            DMA((chunks,)),
            DMA,
            DMA,
            DMA,
            DMA((chips,)),
            DMA((slots,)),
            DMA((slots,)),
            DMA((slots,)),
            DMA((slots,)),
            DMA,
        ],
        compiler_params=pltpu.CompilerParams(
            collective_id=0, has_side_effects=True, vmem_limit_bytes=56 * 1024 * 1024
        ),
        cost_estimate=pl.CostEstimate(
            flops=4 * members * per_dev * BLK * slots * obs_cols,
            bytes_accessed=4 * mem_dev * state_cols * 2,
            transcendentals=0,
        ),
    )(index, tapers, anomalies, obs_anomalies, innovations)


def solution(mesh):
    return jax.shard_map(
        local,
        mesh=mesh,
        in_specs=(
            P("mem", "reg"),
            P("mem", "reg"),
            P("mem", "reg"),
            P("reg", None),
            P("reg", None),
            P(),
        ),
        out_specs=P("mem", "reg"),
        check_vma=False,
    )
```

```python
import functools

import jax
import jax.numpy as jnp
from jax import lax
from jax.experimental import pallas as pl
from jax.experimental.pallas import tpu as pltpu
from jax.sharding import PartitionSpec as P

BLK = 128
REACH = 2
CORES = 2
MESH = pl.DeviceIdType.MESH


def wait_for(ref, sem):
    pltpu.make_async_copy(ref, ref, sem).wait()


def kernel(
    mem_count,
    reg_count,
    chunk,
    slots,
    steps,
    links,
    choice,
    tapers,
    anomalies,
    obs,
    innov,
    out,
    patches,
    window,
    tiles,
    turned,
    weighted,
    results,
    patch_send,
    patch_recv,
    out_send,
    out_recv,
    line_send,
    line_recv,
    pair_send,
    pair_recv,
    plane_send,
    plane_recv,
    tile_sem,
    index_ref,
):
    mem = lax.axis_index("mem")
    reg = lax.axis_index("reg")
    chips = mem_count // CORES
    chip = mem // CORES
    core = lax.rem(mem, CORES)
    twin = chip * CORES + (1 - core)
    mem_dev = anomalies.shape[0]
    chunks = patches.shape[0]
    own_cols = chunks * chunk
    groups = window.shape[5] // BLK
    home = REACH % reg_count
    mem_order = sorted(range(1, mem_count), key=lambda by: abs(by - mem_count // 2))
    mine = pl.ds(pl.multiple_of(mem * mem_dev, mem_dev), mem_dev)

    def device(by):
        return lax.rem(mem + by, mem_count)

    def region(step):
        return lax.rem(reg + step + reg_count, reg_count)

    load = pltpu.make_async_copy(tapers, tiles.at[pl.ds(1, tapers.shape[0])], tile_sem)
    load.start()
    barrier = pltpu.get_barrier_semaphore()
    for by in range(1, mem_count):
        pl.semaphore_signal(barrier, inc=1, device_id=(device(by), reg), device_id_type=MESH)
    for step in steps:
        pl.semaphore_signal(barrier, inc=1, device_id=(mem, region(step)), device_id_type=MESH)
    pl.semaphore_wait(barrier, mem_count - 1 + len(steps))

    def send_patches(c, carry):
        there = patches.at[c, mine]
        for by in mem_order:
            peer = device(by)
            first = pl.multiple_of(peer * own_cols + c * chunk, chunk)
            pltpu.make_async_remote_copy(
                anomalies.at[:, pl.ds(first, chunk)],
                there,
                patch_send,
                patch_recv.at[c],
                device_id=(peer, reg),
                device_id_type=MESH,
            ).start()
        first = pl.multiple_of(mem * own_cols + c * chunk, chunk)
        pltpu.make_async_copy(anomalies.at[:, pl.ds(first, chunk)], there, patch_recv.at[c]).start()
        return carry

    def flipped(mask):
        at = chip
        bit = 1
        while bit < chips:
            if mask & bit:
                at = at + bit * (1 - 2 * lax.rem(at // bit, 2))
            bit *= 2
        return at

    def to_plane(mask):
        for step in steps:
            slot = (REACH - step) % reg_count
            if mask:
                pieces = [window.at[home, :, flipped(mask), core]]
                places = [window.at[slot, :, flipped(mask), core]]
            else:
                pieces = [obs, innov]
                places = [window.at[slot, kind, chip, core] for kind in (0, 1)]
            for piece, place in zip(pieces, places):
                pltpu.make_async_remote_copy(
                    piece,
                    place,
                    plane_send.at[slot],
                    plane_recv.at[slot],
                    device_id=(mem, region(step)),
                    device_id_type=MESH,
                ).start()

    issued = 0
    held = [0]
    fresh = [0]
    for kind, shard in ((0, obs), (1, innov)):
        pltpu.make_async_copy(shard, window.at[home, kind, chip, core], line_recv.at[0]).start()
    bit = chips // 2
    while bit >= 1:
        peer = flipped(bit) * CORES + core
        for mask in held:
            for kind, shard in ((0, obs), (1, innov)):
                there = window.at[home, kind, flipped(mask), core]
                pltpu.make_async_remote_copy(
                    there if mask else shard,
                    there,
                    line_send,
                    line_recv.at[mask + bit],
                    device_id=(peer, reg),
                    device_id_type=MESH,
                ).start()
        for mask in fresh:
            to_plane(mask)
        if issued < chunks:
            send_patches(issued, 0)
            issued += 1
        if bit == chips // 2:
            load.wait()
            tiles[0] = jnp.zeros_like(tiles[0])
            for t in range(tapers.shape[0]):
                tiles[t + 1] = tiles[t + 1] / (mem_count * mem_dev - 1)
        came = [mask + bit for mask in held]
        for mask in came:
            wait_for(window.at[home, :, flipped(mask), core], line_recv.at[mask])
        held = held + came
        fresh = came
        bit //= 2
    wait_for(window.at[home, :, chip, core], line_recv.at[0])
    for mask in fresh:
        to_plane(mask)
    middle = max(issued, chunks * 6 // 8)

    def share(slot):
        return window.at[slot, :, :, core]

    def other(slot):
        return window.at[slot, :, :, 1 - core]

    def to_twin(slot):
        pltpu.make_async_remote_copy(
            share(slot),
            share(slot),
            pair_send.at[slot],
            pair_recv.at[slot],
            device_id=(twin, reg),
            device_id_type=MESH,
        ).start()

    to_twin(home)
    lax.fori_loop(issued, middle, send_patches, 0)
    per_dev = own_cols // BLK

    def list_tiles(b, carry):
        row = mem * per_dev + b
        at = [links[k, row] for k in range(links.shape[0])]
        tile = [choice[k, row] + 1 for k in range(links.shape[0])]
        for w in range((2 * REACH + 1) * groups):
            found = jnp.int32(0)
            for a, t in zip(at, tile):
                found = jnp.where(a == w, t, found)
            index_ref[b, w] = found
        return carry

    lax.fori_loop(0, per_dev, list_tiles, 0)
    for step in steps:
        slot = (REACH - step) % reg_count
        wait_for(share(slot), plane_recv.at[slot])
        to_twin(slot)
    lax.fori_loop(middle, chunks, send_patches, 0)
    for slot in range(slots):
        wait_for(other(slot), pair_recv.at[slot])

    members = mem_count * mem_dev
    rows = min(256, members)
    positions = (2 * REACH + 1) * groups

    def analyse(c, carry):
        wait_for(patches.at[c], patch_recv.at[c])
        turned[...] = patches[c].T
        for slot in range(slots):
            cov = jnp.dot(
                turned[...],
                window[slot, 0].reshape(members, groups * BLK),
                preferred_element_type=jnp.float32,
            )
            for part in range(chunk // BLK):
                for group in range(groups):
                    tile = None
                    for w in range(slot * groups + group, positions, reg_count * groups):
                        one = tiles[index_ref[c * (chunk // BLK) + part, w]]
                        tile = one if tile is None else tile + one
                    piece = cov[part * BLK : (part + 1) * BLK, group * BLK : (group + 1) * BLK]
                    weighted[
                        slot, part * BLK : (part + 1) * BLK, group * BLK : (group + 1) * BLK
                    ] = (piece * tile).astype(jnp.bfloat16)
        flat = [window.at[slot, 1] for slot in range(slots)]
        per_chip = CORES * mem_dev
        for k in range(chips):
            total = None
            for slot in range(slots):
                term = lax.dot_general(
                    flat[slot][k].reshape(per_chip, groups * BLK),
                    weighted[slot],
                    (((1,), (1,)), ((), ())),
                    preferred_element_type=jnp.float32,
                )
                total = term if total is None else total + term
            results[c, k * per_chip : (k + 1) * per_chip, :] = total.astype(jnp.bfloat16)
        there = out.at[:, pl.ds(pl.multiple_of(mem * own_cols + c * chunk, chunk), chunk)]
        for by in mem_order:
            peer = device(by)
            pltpu.make_async_remote_copy(
                results.at[c, pl.ds(pl.multiple_of(peer * mem_dev, mem_dev), mem_dev)],
                there,
                out_send,
                out_recv,
                device_id=(peer, reg),
                device_id_type=MESH,
            ).start()
        pltpu.make_async_copy(results.at[c, mine], there, out_recv).start()
        return carry

    lax.fori_loop(0, chunks, analyse, 0)

    wait_for(out, out_recv)
    sent = pl.ds(0, (mem_count - 1) * own_cols)
    wait_for(anomalies.at[:, sent], patch_send)
    wait_for(out.at[:, sent], out_send)
    wait_for(window.at[home, :, 0 : chips - 1, 0], line_send)
    for slot in range(slots):
        wait_for(share(slot), pair_send.at[slot])
        if slot != home:
            wait_for(share(home), plane_send.at[slot])


def local(anomalies, obs_anomalies, innovations, obs_links, taper_choice, tapers):
    mem_dev, state_cols = anomalies.shape
    mem_count = lax.axis_size("mem")
    reg_count = lax.axis_size("reg")
    members = mem_dev * mem_count
    per_dev = state_cols // BLK // mem_count
    pair = 2 if per_dev % 2 == 0 else 1
    chunk = pair * BLK
    chunks = per_dev // pair
    obs_cols = obs_anomalies.shape[1]
    positions = (2 * REACH + 1) * obs_cols // BLK
    slots = min(2 * REACH + 1, reg_count)
    home = REACH % reg_count
    steps = [(REACH - slot) for slot in range(slots) if slot != home]
    DMA = pltpu.SemaphoreType.DMA
    chips = mem_count // CORES
    return pl.pallas_call(
        functools.partial(kernel, mem_count, reg_count, chunk, slots, steps),
        out_shape=jax.ShapeDtypeStruct((mem_dev, state_cols), jnp.bfloat16),
        in_specs=[
            pl.BlockSpec(memory_space=pltpu.SMEM),
            pl.BlockSpec(memory_space=pltpu.SMEM),
            pl.BlockSpec(memory_space=pltpu.HBM),
            pl.BlockSpec(memory_space=pltpu.HBM),
            pl.BlockSpec(memory_space=pltpu.HBM),
            pl.BlockSpec(memory_space=pltpu.HBM),
        ],
        out_specs=pl.BlockSpec(memory_space=pl.ANY),
        scratch_shapes=[
            pltpu.VMEM((chunks, members, chunk), jnp.bfloat16),
            pltpu.VMEM((slots, 2, chips, CORES, mem_dev, obs_cols), jnp.bfloat16),
            pltpu.VMEM((tapers.shape[0] + 1, BLK, BLK), jnp.float32),
            pltpu.VMEM((chunk, members), jnp.bfloat16),
            pltpu.VMEM((slots, chunk, obs_cols), jnp.bfloat16),
            pltpu.VMEM((chunks, members, chunk), jnp.bfloat16),
            DMA,
            DMA((chunks,)),
            DMA,
            DMA,
            DMA,
            DMA((chips,)),
            DMA((slots,)),
            DMA((slots,)),
            DMA((slots,)),
            DMA((slots,)),
            DMA,
            pltpu.SMEM((per_dev, positions), jnp.int32),
        ],
        compiler_params=pltpu.CompilerParams(
            collective_id=0, has_side_effects=True, vmem_limit_bytes=56 * 1024 * 1024
        ),
        cost_estimate=pl.CostEstimate(
            flops=4 * members * per_dev * BLK * slots * obs_cols,
            bytes_accessed=4 * mem_dev * state_cols * 2,
            transcendentals=0,
        ),
    )(obs_links.T, taper_choice.T, tapers, anomalies, obs_anomalies, innovations)


def solution(mesh):
    return jax.shard_map(
        local,
        mesh=mesh,
        in_specs=(
            P("mem", "reg"),
            P("mem", "reg"),
            P("mem", "reg"),
            P("reg", None),
            P("reg", None),
            P(),
        ),
        out_specs=P("mem", "reg"),
        check_vma=False,
    )
```
